32 devices in a mesh: owner: 8 (over y, x, core), split: 4 (over z).
Axes of the slice: x: 2, y: 2, z: 4, core: 2. Of those that a mesh axis runs over, the one named last changes fastest.
Arguments:
- embeddings: bfloat16 [32768, 1024], P(('owner', 'split')), may hold values from -6 to 6
- row_dest: int32 [32768, 1], P(('owner', 'split')), may hold values from 0 to 39; in each aligned block of 1024 rows (0 to 1023, 1024 to 2047, ...) at most 51 rows name the same one
- row_cluster: int32 [32768], P(('owner', 'split')), may hold values from 0 to 7
Outputs:
- best_similarity: float32 [32768], P(('owner', 'split'))
The draws below stay inside these ranges and needn't reach their ends.
Inputs may be any that keep to these rules, and one draw needn't show every extreme that they name: `row_dest`: among the rows of one source shard no destination is named more than 51 times, a bound that some block reaches.
All inputs are finite; a program needn't handle non-finite values.
Results may differ from the reference program's by a relative error of at most 0.0016.
Values may be sent and summed in bfloat16 or wider, within the bound.
A program may use at most 64 MiB of HBM per device.

```python
import math
import jax
import jax.numpy as jnp
import numpy as np
from jax import lax

D = 1024
CLUSTERS = 8
ROWS_DEV = 1024
NDEST = 40
CAP = 51
ROWS = 32768
DEVICES = 32


def place_ends(array, stream_key, low, largest):
    dims = array.shape
    place = [jax.random.randint(jax.random.fold_in(stream_key, axis), (), 0, dims[axis]) for axis in range(len(dims))]
    array = array.at[tuple(place)].set(low)
    longest = dims.index(max(dims))
    place[longest] = (place[longest] + 1) % dims[longest]
    return array.at[tuple(place)].set(largest)


def block_scale(own_key, extent, pieces, smallest, largest):
    gain, own = 1.0, jax.random.fold_in(own_key, 6)
    for dim, blocks in pieces:
        steps = jnp.exp(jax.random.uniform(jax.random.fold_in(own, dim), (blocks,), jnp.float32, smallest / len(pieces), largest / len(pieces)))
        gain = gain * jnp.repeat(steps, extent[dim] // blocks).reshape([-1 if axis == dim else 1 for axis in range(len(extent))])
    return gain


def assign_block(stream_key, own, number, rows, number_of, top, bound, slope):
    sequence = jax.random.permutation(stream_key, number_of)
    crowded, ordinary = load_shares(number_of, rows * top, bound, slope, True), load_shares(number_of, rows * top, bound, slope, False)
    places = jnp.arange(number_of)

    def named(lengths, offset_by):
        used = int((lengths > 0).sum())
        fixed = max(1, used // 4)
        shifted = fixed + (places - fixed + offset_by * (used - fixed)) % max(1, number_of - fixed)
        return jnp.zeros((number_of,), jnp.int32).at[sequence[jnp.where(places < fixed, places, shifted)]].set(jnp.asarray(lengths, jnp.int32))

    lengths = jnp.where(number % 4 == 0, named(crowded, number // 4), named(ordinary, number - number // 4 - 1))
    mixed = jax.random.permutation(jax.random.fold_in(own, 3), number_of)
    source_of, taker = mixed[0:number_of // 2 * 2:2], mixed[1:number_of // 2 * 2:2]
    slack = jnp.minimum(lengths[source_of] - 1, bound - lengths[taker]) // 2
    slack = jnp.where((source_of == sequence[0]) | (taker == sequence[0]) | (lengths[taker] == 0), 0, jnp.maximum(slack, 0))
    shifted = jax.random.randint(jax.random.fold_in(own, 4), (number_of // 2,), 0, 1 << 20) % (slack + 1)
    lengths = lengths.at[source_of].add(-shifted).at[taker].add(shifted)
    items = jnp.searchsorted(jnp.cumsum(lengths), jnp.arange(rows * top), side="right").astype(jnp.int32)
    table = items.reshape(top, rows).T
    table = table[jax.random.permutation(jax.random.fold_in(own, 1), rows)]
    offset_by = jax.random.randint(jax.random.fold_in(own, 2), (rows, 1), 0, top)
    return jnp.take_along_axis(table, (jnp.arange(top)[None, :] + offset_by) % top, axis=1)


def load_shares(count, total, bound, slope, full):
    weights = [(1 << 20) // math.isqrt(grade ** slope) + 1 for grade in range(1, count + 1)]
    largest = bound if full else min(bound, max(-(-total // count), total * weights[0] // sum(weights)))
    least = 1 if total - largest >= count - 1 else 0
    counts, rest = [largest] + [least] * (count - 1), total - largest - least * (count - 1)
    while rest > 0:
        candidates = [i for i in range(1, count) if counts[i] < largest] or [i for i in range(1, count) if counts[i] < bound]
        pool, left = sum([weights[i] for i in candidates]), rest
        for i in candidates:
            extra = min(bound - counts[i], max(1, left * weights[i] // pool), rest)
            counts[i] = counts[i] + extra
            rest = rest - extra
    return np.array(counts)


def scatter_about(rng, extent, spread, most, pieces=(), held_as=jnp.bfloat16):
    loudness = block_scale(rng, extent, pieces, -0.22, 0.18) if pieces else 1.0
    drawn = jax.random.normal(rng, extent, jnp.float32) * spread * loudness
    return jnp.minimum(jnp.maximum(drawn, -most), most).astype(held_as)


def setup_inputs(seed: int = 0) -> dict:
    streams_of = jax.random.split(jax.random.key(seed), 4)
    embeddings = scatter_about(streams_of[0], (ROWS, D), 1.0, 6.0, ((0, 32),))
    row_dest_keys = jax.random.split(jax.random.fold_in(streams_of[1], 1), ROWS // ROWS_DEV)
    row_dest_turns = jax.random.permutation(jax.random.fold_in(streams_of[1], 3), ROWS // ROWS_DEV)
    row_dest = jax.vmap(lambda own, number: assign_block(jax.random.fold_in(streams_of[1], 2), own, number, ROWS_DEV, NDEST, 1, CAP, 2))(row_dest_keys, row_dest_turns).reshape((ROWS, 1))
    row_cluster = place_ends(jax.random.randint(streams_of[2], (ROWS,), 0, CLUSTERS), jax.random.fold_in(streams_of[2], 1), 0, CLUSTERS - 1).astype(jnp.int32)
    return dict(embeddings=embeddings, row_dest=row_dest, row_cluster=row_cluster)


def unit_rows(embeddings):
    values = embeddings.astype(jnp.float32)
    scale = lax.rsqrt(lax.optimization_barrier(jnp.sum(values * values, axis=1, keepdims=True)) + 1e-06)
    return (values * scale).astype(jnp.bfloat16)

def slot_numbers(destinations):
    targets = jnp.arange(NDEST, dtype=jnp.int32)
    onehot = (destinations[:, None] == targets[None, :]).astype(jnp.int32)
    return lax.optimization_barrier(jnp.sum(onehot * (jnp.cumsum(onehot, axis=0) - 1), axis=1)).astype(jnp.int32)

def reference(embeddings, row_dest, row_cluster):
    unit = unit_rows(embeddings)
    destinations = row_dest[:, 0].reshape(DEVICES, ROWS_DEV)
    slots = jax.vmap(slot_numbers)(destinations)
    sources = jnp.broadcast_to(jnp.arange(DEVICES, dtype=jnp.int32)[:, None], destinations.shape)
    row_ids = jnp.arange(ROWS, dtype=jnp.int32).reshape(DEVICES, ROWS_DEV)
    table = jnp.full((NDEST, DEVICES, CAP), -1, jnp.int32).at[destinations, sources, slots].set(row_ids)
    valid = table >= 0
    safe_ids = jnp.maximum(table, 0)
    is_giant = jnp.arange(NDEST, dtype=jnp.int32) >= DEVICES
    keys = jnp.where(valid, jnp.where(is_giant[:, None, None], 0, row_cluster[safe_ids]), -1)

    def group_best(operands):
        group_ids, group_keys = operands
        flat_ids = jnp.maximum(group_ids.reshape(-1), 0)
        flat_keys = group_keys.reshape(-1)
        rows_here = unit[flat_ids]
        scores = jnp.dot(rows_here, rows_here.T, preferred_element_type=jnp.float32)
        count = flat_keys.shape[0]
        positions = jnp.arange(count, dtype=jnp.int32)
        mask = (flat_keys[:, None] == flat_keys[None, :]) & (flat_keys[:, None] >= 0)
        mask = mask & (positions[:, None] != positions[None, :])
        return lax.optimization_barrier(jnp.max(jnp.where(mask, scores, jnp.float32(-1.0)), axis=1))
    best = lax.map(group_best, (table, keys)).reshape(NDEST, DEVICES, CAP)
    return best[destinations, sources, slots].reshape(ROWS)
```

```python
import functools

import jax
import jax.numpy as jnp
from jax import lax
from jax.experimental import pallas as pl
from jax.experimental.pallas import tpu as pltpu
from jax.sharding import PartitionSpec as P

F32 = jnp.float32
BF16 = jnp.bfloat16
MESH = pl.DeviceIdType.MESH


def kernel(
    sizes, emb_ref, dest_ref, cluster_ref, out_ref,
    unit, send, recv, giant, keycol, keyrow, best, resbuf, resrecv,
    send_sem, recv_sem, giant_sem, res_send_sem, res_recv_sem,
):
    n_owner, n_split, cap, rows, per = sizes
    devices = n_owner * n_split
    ndest = devices + n_owner
    shard, width = emb_ref.shape
    chunk = per * rows
    chunks = devices // per
    my_owner = lax.axis_index("owner")
    my_split = lax.axis_index("split")
    me = my_owner * n_split + my_split

    def holder_split(o):
        return n_split // 2 - 1 + lax.rem(o, 2)

    is_holder = my_split == holder_split(my_owner)

    def coords(d):
        return (lax.div(d, n_split), lax.rem(d, n_split))

    def block(number):
        return pl.ds(pl.multiple_of(number * rows, rows), rows)

    barrier = pltpu.get_barrier_semaphore()

    @pl.loop(1, devices)
    def _(i):
        pl.semaphore_signal(barrier, inc=1, device_id=coords(lax.rem(me + i, devices)), device_id_type=MESH)

    strip = 256

    @pl.loop(0, shard // strip)
    def _(i):
        at = pl.ds(pl.multiple_of(i * strip, strip), strip)
        values = emb_ref[at, :].astype(F32)
        scale = lax.rsqrt(jnp.sum(values * values, axis=1, keepdims=True) + 1e-06)
        unit[at, :] = (values * scale).astype(BF16)

    dest = dest_ref[...]
    gpad = (ndest + 15) // 16 * 16
    onehot = (lax.broadcasted_iota(jnp.int32, (gpad, shard), 0) == dest).astype(F32)
    earlier = (
        lax.broadcasted_iota(jnp.int32, (shard, shard), 0) < lax.broadcasted_iota(jnp.int32, (shard, shard), 1)
    ).astype(F32).astype(BF16)
    before = jnp.dot(onehot.astype(BF16), earlier, preferred_element_type=F32)
    slot = jnp.sum(onehot * before, axis=0, keepdims=True).astype(jnp.int32)
    place = dest * rows + slot
    key = jnp.where(dest < devices, cluster_ref[...], 0) + 1
    slot_hot = (lax.broadcasted_iota(jnp.int32, (128, shard), 0) == slot).astype(F32)
    keymat = lax.dot_general(
        (onehot * key.astype(F32)).astype(BF16), slot_hot.astype(BF16), (((1,), (1,)), ((), ())),
        preferred_element_type=F32,
    )
    keyrow[0:gpad, 0:128] = keymat
    resbuf[...] = jnp.zeros_like(resbuf)

    pl.semaphore_wait(barrier, devices - 1)

    def giant_copy(o):
        target = o * n_split + holder_split(o)
        return target, pltpu.make_async_remote_copy(
            src_ref=send.at[block(devices + o)], dst_ref=giant.at[block(me)],
            send_sem=send_sem.at[devices + o], recv_sem=giant_sem.at[me],
            device_id=coords(target), device_id_type=MESH,
        )

    def local_copy(d):
        return pltpu.make_async_remote_copy(
            src_ref=send.at[block(d)], dst_ref=recv.at[block(me)],
            send_sem=send_sem.at[d], recv_sem=recv_sem.at[me],
            device_id=coords(d), device_id_type=MESH,
        )

    def fill(first):
        wanted = first * rows + lax.broadcasted_iota(jnp.int32, (n_owner * rows, shard), 0)
        pick = (wanted == place).astype(F32).astype(BF16)
        picked = jnp.dot(pick, unit[...], preferred_element_type=F32)
        lane_keys = keyrow[pl.ds(pl.multiple_of(first, 8), n_owner), 0:128]
        marks = jnp.broadcast_to(lane_keys[:, None, :], (n_owner, rows, 128)).reshape(n_owner * rows, 128)
        at_row = lax.broadcasted_iota(jnp.int32, (n_owner * rows, 128), 0) % rows
        head = jnp.where(at_row == cap, marks, picked[:, :128])
        where = pl.ds(pl.multiple_of(first * rows, rows), n_owner * rows)
        send[where, 0:128] = head.astype(BF16)
        send[where, 128:width] = picked[:, 128:].astype(BF16)

    fill(jnp.int32(devices))

    @pl.loop(0, n_owner)
    def _(i):
        o = lax.rem(my_owner + i, n_owner)
        target, copy = giant_copy(o)

        @pl.when(target != me)
        def _():
            copy.start()

        @pl.when(target == me)
        def _():
            giant[block(me), :] = send[block(devices + o), :]

    @pl.loop(0, n_split)
    def _(b):
        group = lax.rem(b + lax.div(me, n_owner), n_split)
        fill(group * n_owner)

        @pl.loop(0, n_owner)
        def _(i):
            d = group * n_owner + lax.rem(me + i, n_owner)

            @pl.when(d != me)
            def _():
                local_copy(d).start()

            @pl.when(d == me)
            def _():
                recv[block(me), :] = send[block(me), :]

    eye = lax.broadcasted_iota(jnp.int32, (rows, 128), 0) == lax.broadcasted_iota(jnp.int32, (rows, 128), 1)

    def group_best(buf, sem, send_first, to_group):
        best[...] = jnp.full_like(best, -1.0)

        def wait_source(q):
            @pl.when(q != me)
            def _():
                pltpu.make_async_remote_copy(
                    src_ref=send.at[block(0)], dst_ref=buf.at[block(q)],
                    send_sem=send_sem.at[0], recv_sem=sem.at[q],
                    device_id=coords(q), device_id_type=MESH,
                ).wait_recv()

        def pairs(ci, cj):
            ri = pl.ds(pl.multiple_of(ci * chunk, chunk), chunk)
            rj = pl.ds(pl.multiple_of(cj * chunk, chunk), chunk)
            scores = lax.dot_general(
                buf[ri, :], buf[rj, :], (((1,), (1,)), ((), ())), preferred_element_type=F32
            )
            ki = keycol[ri, 0:1]
            kj = keyrow[pl.ds(cj * 8, 1), 0:chunk]
            ii = lax.broadcasted_iota(jnp.int32, (chunk, chunk), 0) + (ci - cj) * chunk
            jj = lax.broadcasted_iota(jnp.int32, (chunk, chunk), 1)
            ok = (ki == kj) & (ii != jj)
            top = jnp.max(jnp.where(ok, scores, -1.0), axis=1, keepdims=True)
            best[ri, :] = jnp.maximum(best[ri, :], jnp.broadcast_to(top, (chunk, 128)))

        @pl.loop(0, chunks)
        def _(c):
            @pl.loop(0, per)
            def _(j):
                q = c * per + j
                wait_source(q)
                lane_keys = buf[block(q), 0:128].astype(F32)[cap:cap + 1, :]
                col = jnp.sum(jnp.where(eye, lane_keys, 0.0), axis=1, keepdims=True)
                keycol[block(q), :] = jnp.broadcast_to(col, (rows, 128))

            here = pl.ds(pl.multiple_of(c * chunk, chunk), chunk)
            cols = keycol[here, :]
            turned = jnp.transpose(cols)
            keyrow[pl.ds(pl.multiple_of(c * 8, 8), 8), 0:chunk] = jnp.where(turned[0:8, :] > 0.5, turned[0:8, :], -1.0)
            pairs(c, c)

            @pl.loop(0, c)
            def _(e):
                pairs(c, e)
                pairs(e, c)

        @pl.loop(0, devices)
        def _(i):
            q = lax.rem(me + i, devices)
            line = jnp.sum(jnp.where(eye, best[block(q), :], 0.0), axis=0, keepdims=True)
            resbuf[pl.ds(pl.multiple_of((send_first + q) * 8, 8), 1), :] = line

            @pl.when(q != me)
            def _():
                result_copy(send_first, q, to_group).start()

            @pl.when(q == me)
            def _():
                resrecv[pl.ds(pl.multiple_of(to_group * 8, 8), 8), :] = resbuf[
                    pl.ds(pl.multiple_of((send_first + q) * 8, 8), 8), :
                ]

    def result_copy(send_first, q, group):
        return pltpu.make_async_remote_copy(
            src_ref=resbuf.at[pl.ds(pl.multiple_of((send_first + q) * 8, 8), 8)],
            dst_ref=resrecv.at[pl.ds(pl.multiple_of(group * 8, 8), 8)],
            send_sem=res_send_sem.at[send_first + q], recv_sem=res_recv_sem.at[group],
            device_id=coords(q), device_id_type=MESH,
        )

    @pl.when(is_holder)
    def _():
        group_best(giant, giant_sem, devices, devices + my_owner)

    group_best(recv, recv_sem, 0, me)

    @pl.loop(0, n_owner)
    def _(o):
        target, copy = giant_copy(o)

        @pl.when(target != me)
        def _():
            copy.wait_send()

    @pl.loop(0, devices)
    def _(d):
        @pl.when(d != me)
        def _():
            local_copy(d).wait_send()
            result_copy(0, d, me).wait_send()

            @pl.when(is_holder)
            def _():
                result_copy(devices, d, devices + my_owner).wait_send()

    @pl.loop(0, ndest)
    def _(g):
        o = g - devices
        source = jnp.where(g < devices, g, o * n_split + holder_split(o))

        @pl.when(source != me)
        def _():
            result_copy(0, me, g).wait_recv()

    lines = jnp.concatenate([resrecv[g * 8:g * 8 + 1, :] for g in range(ndest)], axis=0)
    if gpad > ndest:
        lines = jnp.concatenate([lines, jnp.zeros((gpad - ndest, 128), F32)], axis=0)
    dest_again = dest_ref[...]
    hot = (lax.broadcasted_iota(jnp.int32, (gpad, shard), 0) == dest_again).astype(F32)
    found = lax.dot_general(
        lines, hot, (((0,), (0,)), ((), ())), preferred_element_type=F32, precision=lax.Precision.HIGHEST
    )
    out_ref[...] = jnp.sum(jnp.where(slot_hot > 0.5, found, 0.0), axis=0, keepdims=True)


def on_device(embeddings, row_dest, row_cluster):
    n_owner = lax.axis_size("owner")
    n_split = lax.axis_size("split")
    devices = n_owner * n_split
    ndest = devices + n_owner
    shard, width = embeddings.shape
    cap = max(2, 2 * shard // ndest)
    rows = (cap + 1 + 15) // 16 * 16
    per = 1
    while per * 2 <= devices and per * 2 * rows <= 512:
        per *= 2
    chunk = per * rows
    total = devices * rows
    keep = max((ndest + 15) // 16 * 16, devices // per * 8)
    vmem = pl.BlockSpec(memory_space=pltpu.VMEM)
    out = pl.pallas_call(
        functools.partial(kernel, (n_owner, n_split, cap, rows, per)),
        out_shape=jax.ShapeDtypeStruct((1, shard), F32),
        in_specs=[vmem] * 3,
        out_specs=vmem,
        scratch_shapes=[
            pltpu.VMEM((shard, width), BF16),
            pltpu.VMEM((ndest * rows, width), BF16),
            pltpu.VMEM((total, width), BF16),
            pltpu.VMEM((total, width), BF16),
            pltpu.VMEM((total, 128), F32),
            pltpu.VMEM((keep, max(128, chunk)), F32),
            pltpu.VMEM((total, 128), F32),
            pltpu.VMEM((2 * devices * 8, 128), F32),
            pltpu.VMEM((ndest * 8, 128), F32),
            pltpu.SemaphoreType.DMA((ndest,)),
            pltpu.SemaphoreType.DMA((devices,)),
            pltpu.SemaphoreType.DMA((devices,)),
            pltpu.SemaphoreType.DMA((2 * devices,)),
            pltpu.SemaphoreType.DMA((ndest,)),
        ],
        compiler_params=pltpu.CompilerParams(
            collective_id=0, has_side_effects=True, vmem_limit_bytes=56 * 1024 * 1024
        ),
    )(embeddings, row_dest.reshape(1, shard), row_cluster.reshape(1, shard))
    return out.reshape(shard)


def solution(mesh):
    placed = (P(("owner", "split"), None), P(("owner", "split"), None), P(("owner", "split")))
    return jax.shard_map(
        on_device, mesh=mesh, in_specs=placed, out_specs=P(("owner", "split")), check_vma=False
    )
```

```python
import functools

import jax
import jax.numpy as jnp
from jax import lax
from jax.experimental import pallas as pl
from jax.experimental.pallas import tpu as pltpu
from jax.sharding import PartitionSpec as P

F32 = jnp.float32
BF16 = jnp.bfloat16
MESH = pl.DeviceIdType.MESH


def kernel(
    sizes, emb_ref, dest_ref, cluster_ref, out_ref,
    unit, send, recv, giant, keycol, keyrow, best, resbuf, resrecv, *rest
):
    n_owner, n_split, cap, rows, extra, per = sizes
    send_sem, recv_sem, giant_sem, res_send_sem, res_recv_sem = rest[:5]
    if extra:
        send_x, recv_x, giant_x, send_x_sem, recv_x_sem, giant_x_sem = rest[5:]
    else:
        send_x = recv_x = giant_x = send_x_sem = recv_x_sem = giant_x_sem = None
    devices = n_owner * n_split
    ndest = devices + n_owner
    shard, width = emb_ref.shape
    pieces = width // 128
    tall = extra * pieces
    main = per * rows
    chunk = per * (rows + extra)
    pitch = rows + extra
    chunks = devices // per
    my_owner = lax.axis_index("owner")
    my_split = lax.axis_index("split")
    me = my_owner * n_split + my_split

    def holder_split(o):
        return n_split // 2 - 1 + lax.rem(o, 2)

    is_holder = my_split == holder_split(my_owner)

    def coords(d):
        return (lax.div(d, n_split), lax.rem(d, n_split))

    def block(number):
        return pl.ds(pl.multiple_of(number * rows, rows), rows)

    def landing(q):
        at = lax.div(q, per) * chunk + lax.rem(q, per) * rows
        return pl.ds(pl.multiple_of(at, 16), rows)

    def tail(number):
        return pl.ds(pl.multiple_of(number * tall, tall), tall)

    def place_of(index):
        source, at = index // rows, index % rows
        if extra:
            after = index - main
            source = jnp.where(after < 0, source, after // extra)
            at = jnp.where(after < 0, at, rows + after % extra)
        return source, at

    barrier = pltpu.get_barrier_semaphore()

    @pl.loop(1, devices)
    def _(i):
        pl.semaphore_signal(barrier, inc=1, device_id=coords(lax.rem(me + i, devices)), device_id_type=MESH)

    strip = 256

    @pl.loop(0, shard // strip)
    def _(i):
        at = pl.ds(pl.multiple_of(i * strip, strip), strip)
        values = emb_ref[at, :].astype(F32)
        scale = lax.rsqrt(jnp.sum(values * values, axis=1, keepdims=True) + 1e-06)
        unit[at, :] = (values * scale).astype(BF16)

    dest = dest_ref[...]
    gpad = (ndest + 15) // 16 * 16
    onehot = (lax.broadcasted_iota(jnp.int32, (gpad, shard), 0) == dest).astype(F32)
    earlier = (
        lax.broadcasted_iota(jnp.int32, (shard, shard), 0) < lax.broadcasted_iota(jnp.int32, (shard, shard), 1)
    ).astype(F32).astype(BF16)
    before = jnp.dot(onehot.astype(BF16), earlier, preferred_element_type=F32)
    slot = jnp.sum(onehot * before, axis=0, keepdims=True).astype(jnp.int32)
    place = dest * pitch + slot
    key = jnp.where(dest < devices, cluster_ref[...], 0) + 1
    slot_hot = (lax.broadcasted_iota(jnp.int32, (128, shard), 0) == slot).astype(F32)
    keymat = lax.dot_general(
        (onehot * key.astype(F32)).astype(BF16), slot_hot.astype(BF16), (((1,), (1,)), ((), ())),
        preferred_element_type=F32,
    )
    keyrow[0:gpad, 0:128] = keymat
    resbuf[...] = jnp.zeros_like(resbuf)

    pl.semaphore_wait(barrier, devices - 1)

    def row_copies(src, dst, dst_x, sems, sems_x, number, target):
        made = [
            pltpu.make_async_remote_copy(
                src_ref=send.at[block(number)], dst_ref=dst.at[landing(src)],
                send_sem=send_sem.at[number], recv_sem=sems.at[src],
                device_id=coords(target), device_id_type=MESH,
            )
        ]
        if extra:
            made.append(
                pltpu.make_async_remote_copy(
                    src_ref=send_x.at[tail(number)], dst_ref=dst_x.at[tail(src)],
                    send_sem=send_x_sem.at[number], recv_sem=sems_x.at[src],
                    device_id=coords(target), device_id_type=MESH,
                )
            )
        return made

    def giant_copies(o):
        target = o * n_split + holder_split(o)
        return target, row_copies(me, giant, giant_x, giant_sem, giant_x_sem, devices + o, target)

    def local_copies(d):
        return row_copies(me, recv, recv_x, recv_sem, recv_x_sem, d, d)

    def keep_own(number, dst, dst_x):
        dst[landing(me), :] = send[block(number), :]
        if extra:
            dst_x[tail(me), :] = send_x[tail(number), :]

    def select(wanted):
        pick = (wanted == place).astype(F32).astype(BF16)
        return jnp.dot(pick, unit[...], preferred_element_type=F32)

    def fill(first):
        lane_keys = keyrow[pl.ds(pl.multiple_of(first, 8), n_owner), 0:128]
        index = lax.broadcasted_iota(jnp.int32, (n_owner * rows, 1), 0)
        picked = select((first + index // rows) * pitch + index % rows)
        where = pl.ds(pl.multiple_of(first * rows, rows), n_owner * rows)
        if extra:
            send[where, :] = picked.astype(BF16)
            index = lax.broadcasted_iota(jnp.int32, (n_owner * tall, 1), 0)
            picked = select((first + index // tall) * pitch + rows + index % extra)
            piece = index % tall // extra
            laid = picked[:, 0:128]
            for k in range(1, pieces):
                laid = jnp.where(piece == k, picked[:, k * 128:(k + 1) * 128], laid)
            marks = jnp.broadcast_to(lane_keys[:, None, :], (n_owner, tall, 128)).reshape(n_owner * tall, 128)
            laid = jnp.where(index % tall == cap - rows, marks, laid)
            send_x[pl.ds(pl.multiple_of(first * tall, tall), n_owner * tall), :] = laid.astype(BF16)
        else:
            marks = jnp.broadcast_to(lane_keys[:, None, :], (n_owner, rows, 128)).reshape(n_owner * rows, 128)
            head = jnp.where(index % rows == cap, marks, picked[:, :128])
            send[where, 0:128] = head.astype(BF16)
            send[where, 128:width] = picked[:, 128:].astype(BF16)

    fill(jnp.int32(devices))

    @pl.loop(0, n_owner)
    def _(i):
        o = lax.rem(my_owner + i, n_owner)
        target, copies = giant_copies(o)

        @pl.when(target != me)
        def _():
            for copy in copies:
                copy.start()

        @pl.when(target == me)
        def _():
            keep_own(devices + o, giant, giant_x)

    @pl.loop(0, n_split)
    def _(b):
        group = lax.rem(b + lax.div(me, n_owner), n_split)
        fill(group * n_owner)

        @pl.loop(0, n_owner)
        def _(i):
            d = group * n_owner + lax.rem(me + i, n_owner)

            @pl.when(d != me)
            def _():
                for copy in local_copies(d):
                    copy.start()

            @pl.when(d == me)
            def _():
                keep_own(me, recv, recv_x)

    row_source, row_slot = place_of(lax.broadcasted_iota(jnp.int32, (chunk, 1), 0))
    lane_source, _ = place_of(lax.broadcasted_iota(jnp.int32, (1, chunk), 1))
    at_slot = lax.broadcasted_iota(jnp.int32, (chunk, 128), 1) == row_slot
    from_source = (lax.broadcasted_iota(jnp.int32, (max(per, 8), chunk), 0) == lane_source).astype(F32)
    key_rows = per * (tall if extra else rows)
    key_step, key_at = (tall, cap - rows) if extra else (rows, cap)
    key_pick = (
        lax.broadcasted_iota(jnp.int32, (chunk, key_rows), 1) == row_source * key_step + key_at
    ).astype(F32).astype(BF16)
    if extra:
        low = lax.broadcasted_iota(jnp.int32, (per * extra, per * tall), 0)
        high = lax.broadcasted_iota(jnp.int32, (per * extra, per * tall), 1)
        low = low // extra * tall + low % extra

    def group_best(buf, buf_x, sem, sem_x, send_first, to_group):
        best[...] = jnp.full_like(best, -1.0)

        def wait_source(q):
            @pl.when(q != me)
            def _():
                for copy in row_copies(q, buf, buf_x, sem, sem_x, 0, q):
                    copy.wait_recv()

        def pairs(ci, cj):
            ri = pl.ds(pl.multiple_of(ci * chunk, 16), chunk)
            rj = pl.ds(pl.multiple_of(cj * chunk, 16), chunk)
            scores = lax.dot_general(
                buf[ri, :], buf[rj, :], (((1,), (1,)), ((), ())), preferred_element_type=F32
            )
            ki = keycol[ri, 0:1]
            kj = keyrow[pl.ds(cj * 8, 1), 0:chunk]
            ii = lax.broadcasted_iota(jnp.int32, (chunk, chunk), 0) + (ci - cj) * chunk
            jj = lax.broadcasted_iota(jnp.int32, (chunk, chunk), 1)
            ok = (ki == kj) & (ii != jj)
            top = jnp.max(jnp.where(ok, scores, -1.0), axis=1, keepdims=True)
            best[ri, :] = jnp.maximum(best[ri, :], jnp.broadcast_to(top, (chunk, 128)))

        @pl.loop(0, chunks)
        def _(c):
            @pl.loop(0, per)
            def _(j):
                wait_source(c * per + j)

            here = pl.ds(pl.multiple_of(c * chunk, 16), chunk)
            if extra:
                tiles = buf_x[pl.ds(pl.multiple_of(c * key_rows, key_rows), key_rows), :]
                for k in range(pieces):
                    gather = (high == low + k * extra).astype(F32).astype(BF16)
                    buf[pl.ds(pl.multiple_of(c * chunk + main, 16), per * extra), k * 128:(k + 1) * 128] = jnp.dot(
                        gather, tiles, preferred_element_type=F32
                    ).astype(BF16)
            else:
                tiles = buf[here, 0:128]
            lane_keys = jnp.dot(key_pick, tiles, preferred_element_type=F32)
            col = jnp.sum(jnp.where(at_slot, lane_keys, 0.0), axis=1, keepdims=True)
            cols = jnp.broadcast_to(col, (chunk, 128))
            keycol[here, :] = cols
            turned = jnp.transpose(cols)
            keyrow[pl.ds(pl.multiple_of(c * 8, 8), 8), 0:chunk] = jnp.where(turned[0:8, :] > 0.5, turned[0:8, :], -1.0)
            pairs(c, c)

            @pl.loop(0, c)
            def _(e):
                pairs(c, e)
                pairs(e, c)

        @pl.loop(0, chunks)
        def _(c):
            here = pl.ds(pl.multiple_of(c * chunk, 16), chunk)
            lines = jnp.dot(
                from_source, jnp.where(at_slot, best[here, :], 0.0),
                preferred_element_type=F32, precision=lax.Precision.HIGHEST,
            )
            for j in range(per):
                resbuf[pl.ds(pl.multiple_of((send_first + c * per + j) * 8, 8), 1), :] = lines[j:j + 1, :]

            @pl.loop(0, per)
            def _(j):
                q = c * per + j

                @pl.when(q != me)
                def _():
                    result_copy(send_first, q, to_group).start()

                @pl.when(q == me)
                def _():
                    resrecv[pl.ds(pl.multiple_of(to_group * 8, 8), 8), :] = resbuf[
                        pl.ds(pl.multiple_of((send_first + q) * 8, 8), 8), :
                    ]

    def result_copy(send_first, q, group):
        return pltpu.make_async_remote_copy(
            src_ref=resbuf.at[pl.ds(pl.multiple_of((send_first + q) * 8, 8), 8)],
            dst_ref=resrecv.at[pl.ds(pl.multiple_of(group * 8, 8), 8)],
            send_sem=res_send_sem.at[send_first + q], recv_sem=res_recv_sem.at[group],
            device_id=coords(q), device_id_type=MESH,
        )

    @pl.when(is_holder)
    def _():
        group_best(giant, giant_x, giant_sem, giant_x_sem, devices, devices + my_owner)

    group_best(recv, recv_x, recv_sem, recv_x_sem, 0, me)

    @pl.loop(0, n_owner)
    def _(o):
        target, copies = giant_copies(o)

        @pl.when(target != me)
        def _():
            for copy in copies:
                copy.wait_send()

    @pl.loop(0, devices)
    def _(d):
        @pl.when(d != me)
        def _():
            for copy in local_copies(d):
                copy.wait_send()
            result_copy(0, d, me).wait_send()

            @pl.when(is_holder)
            def _():
                result_copy(devices, d, devices + my_owner).wait_send()

    @pl.loop(0, ndest)
    def _(g):
        o = g - devices
        source = jnp.where(g < devices, g, o * n_split + holder_split(o))

        @pl.when(source != me)
        def _():
            result_copy(0, me, g).wait_recv()

    lines = jnp.concatenate([resrecv[g * 8:g * 8 + 1, :] for g in range(ndest)], axis=0)
    if gpad > ndest:
        lines = jnp.concatenate([lines, jnp.zeros((gpad - ndest, 128), F32)], axis=0)
    dest_again = dest_ref[...]
    hot = (lax.broadcasted_iota(jnp.int32, (gpad, shard), 0) == dest_again).astype(F32)
    found = lax.dot_general(
        lines, hot, (((0,), (0,)), ((), ())), preferred_element_type=F32, precision=lax.Precision.HIGHEST
    )
    out_ref[...] = jnp.sum(jnp.where(slot_hot > 0.5, found, 0.0), axis=0, keepdims=True)


def on_device(embeddings, row_dest, row_cluster):
    n_owner = lax.axis_size("owner")
    n_split = lax.axis_size("split")
    devices = n_owner * n_split
    ndest = devices + n_owner
    shard, width = embeddings.shape
    cap = max(2, 2 * shard // ndest)
    rows, extra = cap // 16 * 16, cap + 1 - cap // 16 * 16
    extra += extra % 2
    if rows == 0 or extra > 8 or extra * (width // 128) % 16:
        rows, extra = (cap + 1 + 15) // 16 * 16, 0
    tall = extra * (width // 128)
    per = 1
    while per * 2 <= devices and per * 2 * (rows + extra) <= 512:
        per *= 2
    chunk = per * (rows + extra)
    total = devices * (rows + extra)
    keep = max((ndest + 15) // 16 * 16, devices // per * 8)
    vmem = pl.BlockSpec(memory_space=pltpu.VMEM)
    tails = []
    if extra:
        tails = [
            pltpu.VMEM((ndest * tall, 128), BF16),
            pltpu.VMEM((devices * tall, 128), BF16),
            pltpu.VMEM((devices * tall, 128), BF16),
            pltpu.SemaphoreType.DMA((ndest,)),
            pltpu.SemaphoreType.DMA((devices,)),
            pltpu.SemaphoreType.DMA((devices,)),
        ]
    out = pl.pallas_call(
        functools.partial(kernel, (n_owner, n_split, cap, rows, extra, per)),
        out_shape=jax.ShapeDtypeStruct((1, shard), F32),
        in_specs=[vmem] * 3,
        out_specs=vmem,
        scratch_shapes=[
            pltpu.VMEM((shard, width), BF16),
            pltpu.VMEM((ndest * rows, width), BF16),
            pltpu.VMEM((total, width), BF16),
            pltpu.VMEM((total, width), BF16),
            pltpu.VMEM((total, 128), F32),
            pltpu.VMEM((keep, max(128, chunk)), F32),
            pltpu.VMEM((total, 128), F32),
            pltpu.VMEM((2 * devices * 8, 128), F32),
            pltpu.VMEM((ndest * 8, 128), F32),
            pltpu.SemaphoreType.DMA((ndest,)),
            pltpu.SemaphoreType.DMA((devices,)),
            pltpu.SemaphoreType.DMA((devices,)),
            pltpu.SemaphoreType.DMA((2 * devices,)),
            pltpu.SemaphoreType.DMA((ndest,)),
        ] + tails,
        compiler_params=pltpu.CompilerParams(
            collective_id=0, has_side_effects=True, vmem_limit_bytes=56 * 1024 * 1024
        ),
    )(embeddings, row_dest.reshape(1, shard), row_cluster.reshape(1, shard))
    return out.reshape(shard)


def solution(mesh):
    placed = (P(("owner", "split"), None), P(("owner", "split"), None), P(("owner", "split")))
    return jax.shard_map(
        on_device, mesh=mesh, in_specs=placed, out_specs=P(("owner", "split")), check_vma=False
    )
```

```python
import functools

import jax
import jax.numpy as jnp
from jax import lax
from jax.experimental import pallas as pl
from jax.experimental.pallas import tpu as pltpu
from jax.sharding import PartitionSpec as P

F32 = jnp.float32
BF16 = jnp.bfloat16
MESH = pl.DeviceIdType.MESH


def kernel(
    sizes, emb_ref, dest_ref, cluster_ref, out_ref,
    unit, send, recv, giant, keycol, keyrow, best, resbuf, resrecv, *rest
):
    n_owner, n_split, cap, rows, extra, per = sizes
    send_sem, recv_sem, giant_sem, res_send_sem, res_recv_sem = rest[:5]
    if extra:
        send_x, recv_x, giant_x, send_x_sem, recv_x_sem, giant_x_sem = rest[5:]
    else:
        send_x = recv_x = giant_x = send_x_sem = recv_x_sem = giant_x_sem = None
    devices = n_owner * n_split
    ndest = devices + n_owner
    shard, width = emb_ref.shape
    pieces = width // 128
    tall = extra * pieces
    main = per * rows
    chunk = per * (rows + extra)
    pitch = rows + extra
    chunks = devices // per
    my_owner = lax.axis_index("owner")
    my_split = lax.axis_index("split")
    me = my_split * n_owner + my_owner

    def walk(start, step, count):
        if count % 2:
            return lax.rem(start + step, count)
        half = count // 2
        side = lax.rem(lax.div(start, half) + lax.div(step, half), 2)
        return side * half + lax.rem(lax.rem(start, half) + lax.rem(step, half), half)

    def holder_split(o):
        return n_split // 2 - 1 + lax.rem(o, 2)

    is_holder = my_split == holder_split(my_owner)

    def coords(d):
        return (lax.rem(d, n_owner), lax.div(d, n_owner))

    def block(number):
        return pl.ds(pl.multiple_of(number * rows, rows), rows)

    def landing(q):
        at = lax.div(q, per) * chunk + lax.rem(q, per) * rows
        return pl.ds(pl.multiple_of(at, 16), rows)

    def tail(number):
        return pl.ds(pl.multiple_of(number * tall, tall), tall)

    def place_of(index):
        source, at = index // rows, index % rows
        if extra:
            after = index - main
            source = jnp.where(after < 0, source, after // extra)
            at = jnp.where(after < 0, at, rows + after % extra)
        return source, at

    barrier = pltpu.get_barrier_semaphore()

    @pl.loop(1, devices)
    def _(i):
        pl.semaphore_signal(barrier, inc=1, device_id=coords(lax.rem(me + i, devices)), device_id_type=MESH)

    strip = 256

    @pl.loop(0, shard // strip)
    def _(i):
        at = pl.ds(pl.multiple_of(i * strip, strip), strip)
        values = emb_ref[at, :].astype(F32)
        scale = lax.rsqrt(jnp.sum(values * values, axis=1, keepdims=True) + 1e-06)
        unit[at, :] = (values * scale).astype(BF16)

    def renumbered():
        named = dest_ref[...]
        return jnp.where(named < devices, named % n_split * n_owner + named // n_split, named)

    dest = renumbered()
    gpad = (ndest + 15) // 16 * 16
    onehot = (lax.broadcasted_iota(jnp.int32, (gpad, shard), 0) == dest).astype(F32)
    span = 128
    earlier = (
        lax.broadcasted_iota(jnp.int32, (span, span), 0) < lax.broadcasted_iota(jnp.int32, (span, span), 1)
    ).astype(F32).astype(BF16)
    seen = jnp.zeros((gpad, 1), F32)
    counts = []
    for k in range(0, shard, span):
        part = onehot[:, k:k + span]
        counts.append(seen + jnp.dot(part.astype(BF16), earlier, preferred_element_type=F32))
        seen = seen + jnp.sum(part, axis=1, keepdims=True)
    before = jnp.concatenate(counts, axis=1)
    slot = jnp.sum(onehot * before, axis=0, keepdims=True).astype(jnp.int32)
    place = dest * pitch + slot
    key = jnp.where(dest < devices, cluster_ref[...], 0) + 1
    slot_hot = (lax.broadcasted_iota(jnp.int32, (128, shard), 0) == slot).astype(F32)
    keymat = lax.dot_general(
        (onehot * key.astype(F32)).astype(BF16), slot_hot.astype(BF16), (((1,), (1,)), ((), ())),
        preferred_element_type=F32,
    )
    keyrow[0:gpad, 0:128] = keymat
    resbuf[...] = jnp.zeros_like(resbuf)

    pl.semaphore_wait(barrier, devices - 1)

    def row_copies(src, dst, dst_x, sems, sems_x, number, target):
        made = [
            pltpu.make_async_remote_copy(
                src_ref=send.at[block(number)], dst_ref=dst.at[landing(src)],
                send_sem=send_sem.at[number], recv_sem=sems.at[src],
                device_id=coords(target), device_id_type=MESH,
            )
        ]
        if extra:
            made.append(
                pltpu.make_async_remote_copy(
                    src_ref=send_x.at[tail(number)], dst_ref=dst_x.at[tail(src)],
                    send_sem=send_x_sem.at[number], recv_sem=sems_x.at[src],
                    device_id=coords(target), device_id_type=MESH,
                )
            )
        return made

    def giant_copies(o):
        target = holder_split(o) * n_owner + o
        return target, row_copies(me, giant, giant_x, giant_sem, giant_x_sem, devices + o, target)

    def local_copies(d):
        return row_copies(me, recv, recv_x, recv_sem, recv_x_sem, d, d)

    def keep_own(number, dst, dst_x):
        dst[landing(me), :] = send[block(number), :]
        if extra:
            dst_x[tail(me), :] = send_x[tail(number), :]

    def select(wanted):
        pick = (wanted == place).astype(F32).astype(BF16)
        return jnp.dot(pick, unit[...], preferred_element_type=F32)

    def fill(first):
        lane_keys = keyrow[pl.ds(pl.multiple_of(first, 8), n_owner), 0:128]
        index = lax.broadcasted_iota(jnp.int32, (n_owner * rows, 1), 0)
        picked = select((first + index // rows) * pitch + index % rows)
        where = pl.ds(pl.multiple_of(first * rows, rows), n_owner * rows)
        if extra:
            send[where, :] = picked.astype(BF16)
            index = lax.broadcasted_iota(jnp.int32, (n_owner * tall, 1), 0)
            picked = select((first + index // tall) * pitch + rows + index % extra)
            piece = index % tall // extra
            laid = picked[:, 0:128]
            for k in range(1, pieces):
                laid = jnp.where(piece == k, picked[:, k * 128:(k + 1) * 128], laid)
            marks = jnp.broadcast_to(lane_keys[:, None, :], (n_owner, tall, 128)).reshape(n_owner * tall, 128)
            laid = jnp.where(index % tall == cap - rows, marks, laid)
            send_x[pl.ds(pl.multiple_of(first * tall, tall), n_owner * tall), :] = laid.astype(BF16)
        else:
            marks = jnp.broadcast_to(lane_keys[:, None, :], (n_owner, rows, 128)).reshape(n_owner * rows, 128)
            head = jnp.where(index % rows == cap, marks, picked[:, :128])
            send[where, 0:128] = head.astype(BF16)
            send[where, 128:width] = picked[:, 128:].astype(BF16)

    fill(jnp.int32(devices))

    @pl.loop(0, n_owner)
    def _(i):
        o = lax.rem(my_owner + i, n_owner)
        target, copies = giant_copies(o)

        @pl.when(target != me)
        def _():
            for copy in copies:
                copy.start()

        @pl.when(target == me)
        def _():
            keep_own(devices + o, giant, giant_x)

    @pl.loop(0, n_split)
    def _(b):
        group = walk(my_split, b, n_split)
        fill(group * n_owner)

        @pl.loop(0, n_owner)
        def _(i):
            d = group * n_owner + lax.rem(me + i, n_owner)

            @pl.when(d != me)
            def _():
                for copy in local_copies(d):
                    copy.start()

            @pl.when(d == me)
            def _():
                keep_own(me, recv, recv_x)

    row_source, row_slot = place_of(lax.broadcasted_iota(jnp.int32, (chunk, 1), 0))
    lane_source, _ = place_of(lax.broadcasted_iota(jnp.int32, (1, chunk), 1))
    at_slot = lax.broadcasted_iota(jnp.int32, (chunk, 128), 1) == row_slot
    from_source = (lax.broadcasted_iota(jnp.int32, (max(per, 8), chunk), 0) == lane_source).astype(F32)
    key_rows = per * (tall if extra else rows)
    key_step, key_at = (tall, cap - rows) if extra else (rows, cap)
    key_pick = (
        lax.broadcasted_iota(jnp.int32, (chunk, key_rows), 1) == row_source * key_step + key_at
    ).astype(F32).astype(BF16)
    if extra:
        low = lax.broadcasted_iota(jnp.int32, (per * extra, per * tall), 0)
        high = lax.broadcasted_iota(jnp.int32, (per * extra, per * tall), 1)
        low = low // extra * tall + low % extra

    def group_best(buf, buf_x, sem, sem_x, send_first, to_group):
        best[...] = jnp.full_like(best, -1.0)

        def wait_source(q):
            @pl.when(q != me)
            def _():
                for copy in row_copies(q, buf, buf_x, sem, sem_x, 0, q):
                    copy.wait_recv()

        def pairs(ci, cj):
            ri = pl.ds(pl.multiple_of(ci * chunk, 16), chunk)
            rj = pl.ds(pl.multiple_of(cj * chunk, 16), chunk)
            scores = lax.dot_general(
                buf[ri, :], buf[rj, :], (((1,), (1,)), ((), ())), preferred_element_type=F32
            )
            ki = keycol[ri, 0:1]
            kj = keyrow[pl.ds(cj * 8, 1), 0:chunk]
            ii = lax.broadcasted_iota(jnp.int32, (chunk, chunk), 0) + (ci - cj) * chunk
            jj = lax.broadcasted_iota(jnp.int32, (chunk, chunk), 1)
            ok = (ki == kj) & (ii != jj)
            top = jnp.max(jnp.where(ok, scores, -1.0), axis=1, keepdims=True)
            best[ri, :] = jnp.maximum(best[ri, :], jnp.broadcast_to(top, (chunk, 128)))

        my_chunk = lax.div(me, per)

        @pl.loop(0, chunks)
        def _(step):
            c = walk(my_chunk, step, chunks)

            @pl.loop(0, per)
            def _(j):
                wait_source(c * per + j)

            here = pl.ds(pl.multiple_of(c * chunk, 16), chunk)
            if extra:
                tiles = buf_x[pl.ds(pl.multiple_of(c * key_rows, key_rows), key_rows), :]
                for k in range(pieces):
                    gather = (high == low + k * extra).astype(F32).astype(BF16)
                    buf[pl.ds(pl.multiple_of(c * chunk + main, 16), per * extra), k * 128:(k + 1) * 128] = jnp.dot(
                        gather, tiles, preferred_element_type=F32
                    ).astype(BF16)
            else:
                tiles = buf[here, 0:128]
            lane_keys = jnp.dot(key_pick, tiles, preferred_element_type=F32)
            col = jnp.sum(jnp.where(at_slot, lane_keys, 0.0), axis=1, keepdims=True)
            cols = jnp.broadcast_to(col, (chunk, 128))
            keycol[here, :] = cols
            turned = jnp.transpose(cols)
            keyrow[pl.ds(pl.multiple_of(c * 8, 8), 8), 0:chunk] = jnp.where(turned[0:8, :] > 0.5, turned[0:8, :], -1.0)
            pairs(c, c)

            @pl.loop(0, step)
            def _(done):
                e = walk(my_chunk, done, chunks)
                pairs(c, e)
                pairs(e, c)

        @pl.loop(0, chunks)
        def _(c):
            here = pl.ds(pl.multiple_of(c * chunk, 16), chunk)
            lines = jnp.dot(
                from_source, jnp.where(at_slot, best[here, :], 0.0),
                preferred_element_type=F32, precision=lax.Precision.HIGHEST,
            )
            for j in range(per):
                resbuf[pl.ds(pl.multiple_of((send_first + c * per + j) * 8, 8), 1), :] = lines[j:j + 1, :]

            @pl.loop(0, per)
            def _(j):
                q = c * per + j

                @pl.when(q != me)
                def _():
                    result_copy(send_first, q, to_group).start()

                @pl.when(q == me)
                def _():
                    resrecv[pl.ds(pl.multiple_of(to_group * 8, 8), 8), :] = resbuf[
                        pl.ds(pl.multiple_of((send_first + q) * 8, 8), 8), :
                    ]

    def result_copy(send_first, q, group):
        return pltpu.make_async_remote_copy(
            src_ref=resbuf.at[pl.ds(pl.multiple_of((send_first + q) * 8, 8), 8)],
            dst_ref=resrecv.at[pl.ds(pl.multiple_of(group * 8, 8), 8)],
            send_sem=res_send_sem.at[send_first + q], recv_sem=res_recv_sem.at[group],
            device_id=coords(q), device_id_type=MESH,
        )

    @pl.when(is_holder)
    def _():
        group_best(giant, giant_x, giant_sem, giant_x_sem, devices, devices + my_owner)

    group_best(recv, recv_x, recv_sem, recv_x_sem, 0, me)

    @pl.loop(0, n_owner)
    def _(o):
        target, copies = giant_copies(o)

        @pl.when(target != me)
        def _():
            for copy in copies:
                copy.wait_send()

    @pl.loop(0, devices)
    def _(d):
        @pl.when(d != me)
        def _():
            for copy in local_copies(d):
                copy.wait_send()
            result_copy(0, d, me).wait_send()

            @pl.when(is_holder)
            def _():
                result_copy(devices, d, devices + my_owner).wait_send()

    @pl.loop(0, ndest)
    def _(g):
        o = g - devices
        source = jnp.where(g < devices, g, holder_split(o) * n_owner + o)

        @pl.when(source != me)
        def _():
            result_copy(0, me, g).wait_recv()

    lines = jnp.concatenate([resrecv[g * 8:g * 8 + 1, :] for g in range(ndest)], axis=0)
    if gpad > ndest:
        lines = jnp.concatenate([lines, jnp.zeros((gpad - ndest, 128), F32)], axis=0)
    dest_again = renumbered()
    hot = (lax.broadcasted_iota(jnp.int32, (gpad, shard), 0) == dest_again).astype(F32)
    found = lax.dot_general(
        lines, hot, (((0,), (0,)), ((), ())), preferred_element_type=F32, precision=lax.Precision.HIGHEST
    )
    out_ref[...] = jnp.sum(jnp.where(slot_hot > 0.5, found, 0.0), axis=0, keepdims=True)


def on_device(embeddings, row_dest, row_cluster):
    n_owner = lax.axis_size("owner")
    n_split = lax.axis_size("split")
    devices = n_owner * n_split
    ndest = devices + n_owner
    shard, width = embeddings.shape
    cap = max(2, 2 * shard // ndest)
    rows, extra = cap // 16 * 16, cap + 1 - cap // 16 * 16
    extra += extra % 2
    if rows == 0 or extra > 8 or extra * (width // 128) % 16:
        rows, extra = (cap + 1 + 15) // 16 * 16, 0
    tall = extra * (width // 128)
    per = 1
    while per * 2 <= devices and per * 2 * (rows + extra) <= 512:
        per *= 2
    chunk = per * (rows + extra)
    total = devices * (rows + extra)
    keep = max((ndest + 15) // 16 * 16, devices // per * 8)
    vmem = pl.BlockSpec(memory_space=pltpu.VMEM)
    tails = []
    if extra:
        tails = [
            pltpu.VMEM((ndest * tall, 128), BF16),
            pltpu.VMEM((devices * tall, 128), BF16),
            pltpu.VMEM((devices * tall, 128), BF16),
            pltpu.SemaphoreType.DMA((ndest,)),
            pltpu.SemaphoreType.DMA((devices,)),
            pltpu.SemaphoreType.DMA((devices,)),
        ]
    out = pl.pallas_call(
        functools.partial(kernel, (n_owner, n_split, cap, rows, extra, per)),
        out_shape=jax.ShapeDtypeStruct((1, shard), F32),
        in_specs=[vmem] * 3,
        out_specs=vmem,
        scratch_shapes=[
            pltpu.VMEM((shard, width), BF16),
            pltpu.VMEM((ndest * rows, width), BF16),
            pltpu.VMEM((total, width), BF16),
            pltpu.VMEM((total, width), BF16),
            pltpu.VMEM((total, 128), F32),
            pltpu.VMEM((keep, max(128, chunk)), F32),
            pltpu.VMEM((total, 128), F32),
            pltpu.VMEM((2 * devices * 8, 128), F32),
            pltpu.VMEM((ndest * 8, 128), F32),
            pltpu.SemaphoreType.DMA((ndest,)),
            pltpu.SemaphoreType.DMA((devices,)),
            pltpu.SemaphoreType.DMA((devices,)),
            pltpu.SemaphoreType.DMA((2 * devices,)),
            pltpu.SemaphoreType.DMA((ndest,)),
        ] + tails,
        compiler_params=pltpu.CompilerParams(
            collective_id=0, has_side_effects=True, vmem_limit_bytes=56 * 1024 * 1024
        ),
    )(embeddings, row_dest.reshape(1, shard), row_cluster.reshape(1, shard))
    return out.reshape(shard)


def solution(mesh):
    placed = (P(("owner", "split"), None), P(("owner", "split"), None), P(("owner", "split")))
    return jax.shard_map(
        on_device, mesh=mesh, in_specs=placed, out_specs=P(("owner", "split")), check_vma=False
    )
```

```python
import functools

import jax
import jax.numpy as jnp
from jax import lax
from jax.experimental import pallas as pl
from jax.experimental.pallas import tpu as pltpu
from jax.sharding import PartitionSpec as P

F32 = jnp.float32
BF16 = jnp.bfloat16
MESH = pl.DeviceIdType.MESH


def kernel(
    sizes, emb_ref, dest_ref, cluster_ref, out_ref,
    unit, send, recv, giant, keycol, keyrow, best, resbuf, resrecv, *rest
):
    n_owner, n_split, cap, rows, extra, per = sizes
    send_sem, recv_sem, giant_sem, res_send_sem, res_recv_sem = rest[:5]
    if extra:
        send_x, recv_x, giant_x, send_x_sem, recv_x_sem, giant_x_sem = rest[5:]
    else:
        send_x = recv_x = giant_x = send_x_sem = recv_x_sem = giant_x_sem = None
    devices = n_owner * n_split
    ndest = devices + n_owner
    shard, width = emb_ref.shape
    pieces = width // 128
    tall = extra * pieces
    main = per * rows
    chunk = per * (rows + extra)
    pitch = rows + extra
    chunks = devices // per
    my_owner = lax.axis_index("owner")
    my_split = lax.axis_index("split")
    me = my_split * n_owner + my_owner

    def walk(start, step, count):
        if count % 2:
            return lax.rem(start + step, count)
        half = count // 2
        side = lax.rem(lax.div(start, half) + lax.div(step, half), 2)
        return side * half + lax.rem(lax.rem(start, half) + lax.rem(step, half), half)

    def holder_split(o):
        return n_split // 2 - 1 + lax.rem(o, 2)

    is_holder = my_split == holder_split(my_owner)

    def coords(d):
        return (lax.rem(d, n_owner), lax.div(d, n_owner))

    def block(number):
        return pl.ds(pl.multiple_of(number * rows, rows), rows)

    def landing(q):
        at = lax.div(q, per) * chunk + lax.rem(q, per) * rows
        return pl.ds(pl.multiple_of(at, 16), rows)

    def tail(number):
        return pl.ds(pl.multiple_of(number * tall, tall), tall)

    def place_of(index):
        source, at = index // rows, index % rows
        if extra:
            after = index - main
            source = jnp.where(after < 0, source, after // extra)
            at = jnp.where(after < 0, at, rows + after % extra)
        return source, at

    barrier = pltpu.get_barrier_semaphore()

    @pl.loop(1, devices)
    def _(i):
        pl.semaphore_signal(barrier, inc=1, device_id=coords(lax.rem(me + i, devices)), device_id_type=MESH)

    strip = 256

    @pl.loop(0, shard // strip)
    def _(i):
        at = pl.ds(pl.multiple_of(i * strip, strip), strip)
        values = emb_ref[at, :].astype(F32)
        scale = lax.rsqrt(jnp.sum(values * values, axis=1, keepdims=True) + 1e-06)
        unit[at, :] = (values * scale).astype(BF16)

    def renumbered():
        named = dest_ref[...]
        return jnp.where(named < devices, named % n_split * n_owner + named // n_split, named)

    dest = renumbered()
    gpad = (ndest + 15) // 16 * 16
    onehot = (lax.broadcasted_iota(jnp.int32, (gpad, shard), 0) == dest).astype(F32)
    span = 128
    earlier = (
        lax.broadcasted_iota(jnp.int32, (span, span), 0) < lax.broadcasted_iota(jnp.int32, (span, span), 1)
    ).astype(F32).astype(BF16)
    seen = jnp.zeros((gpad, 1), F32)
    counts = []
    for k in range(0, shard, span):
        part = onehot[:, k:k + span]
        counts.append(seen + jnp.dot(part.astype(BF16), earlier, preferred_element_type=F32))
        seen = seen + jnp.sum(part, axis=1, keepdims=True)
    before = jnp.concatenate(counts, axis=1)
    slot = jnp.sum(onehot * before, axis=0, keepdims=True).astype(jnp.int32)
    place = dest * pitch + slot
    key = jnp.where(dest < devices, cluster_ref[...], 0) + 1
    slot_hot = (lax.broadcasted_iota(jnp.int32, (128, shard), 0) == slot).astype(F32)
    keymat = lax.dot_general(
        (onehot * key.astype(F32)).astype(BF16), slot_hot.astype(BF16), (((1,), (1,)), ((), ())),
        preferred_element_type=F32,
    )
    keyrow[0:gpad, 0:128] = keymat
    resbuf[...] = jnp.zeros_like(resbuf)

    pl.semaphore_wait(barrier, devices - 1)

    def row_copies(src, dst, dst_x, sems, sems_x, number, target):
        made = [
            pltpu.make_async_remote_copy(
                src_ref=send.at[block(number)], dst_ref=dst.at[landing(src)],
                send_sem=send_sem.at[number], recv_sem=sems.at[src],
                device_id=coords(target), device_id_type=MESH,
            )
        ]
        if extra:
            made.append(
                pltpu.make_async_remote_copy(
                    src_ref=send_x.at[tail(number)], dst_ref=dst_x.at[tail(src)],
                    send_sem=send_x_sem.at[number], recv_sem=sems_x.at[src],
                    device_id=coords(target), device_id_type=MESH,
                )
            )
        return made

    def giant_copies(o):
        target = holder_split(o) * n_owner + o
        return target, row_copies(me, giant, giant_x, giant_sem, giant_x_sem, devices + o, target)

    def local_copies(d):
        return row_copies(me, recv, recv_x, recv_sem, recv_x_sem, d, d)

    def keep_own(number, dst, dst_x):
        dst[landing(me), :] = send[block(number), :]
        if extra:
            dst_x[tail(me), :] = send_x[tail(number), :]

    def select(wanted):
        pick = (wanted == place).astype(F32).astype(BF16)
        return jnp.dot(pick, unit[...], preferred_element_type=F32)

    def fill(first):
        lane_keys = keyrow[pl.ds(pl.multiple_of(first, 8), n_owner), 0:128]
        index = lax.broadcasted_iota(jnp.int32, (n_owner * rows, 1), 0)
        picked = select((first + index // rows) * pitch + index % rows)
        where = pl.ds(pl.multiple_of(first * rows, rows), n_owner * rows)
        if extra:
            send[where, :] = picked.astype(BF16)
            index = lax.broadcasted_iota(jnp.int32, (n_owner * tall, 1), 0)
            picked = select((first + index // tall) * pitch + rows + index % extra)
            piece = index % tall // extra
            laid = picked[:, 0:128]
            for k in range(1, pieces):
                laid = jnp.where(piece == k, picked[:, k * 128:(k + 1) * 128], laid)
            marks = jnp.broadcast_to(lane_keys[:, None, :], (n_owner, tall, 128)).reshape(n_owner * tall, 128)
            laid = jnp.where(index % tall == cap - rows, marks, laid)
            send_x[pl.ds(pl.multiple_of(first * tall, tall), n_owner * tall), :] = laid.astype(BF16)
        else:
            marks = jnp.broadcast_to(lane_keys[:, None, :], (n_owner, rows, 128)).reshape(n_owner * rows, 128)
            head = jnp.where(index % rows == cap, marks, picked[:, :128])
            send[where, 0:128] = head.astype(BF16)
            send[where, 128:width] = picked[:, 128:].astype(BF16)

    fill(jnp.int32(devices))

    @pl.loop(0, n_owner)
    def _(i):
        o = lax.rem(my_owner + i, n_owner)
        target, copies = giant_copies(o)

        @pl.when(target != me)
        def _():
            for copy in copies:
                copy.start()

        @pl.when(target == me)
        def _():
            keep_own(devices + o, giant, giant_x)

    @pl.loop(0, n_split)
    def _(b):
        group = walk(my_split, b, n_split)
        fill(group * n_owner)

        @pl.loop(0, n_owner)
        def _(i):
            d = group * n_owner + lax.rem(me + i, n_owner)

            @pl.when(d != me)
            def _():
                for copy in local_copies(d):
                    copy.start()

            @pl.when(d == me)
            def _():
                keep_own(me, recv, recv_x)

    row_source, row_slot = place_of(lax.broadcasted_iota(jnp.int32, (chunk, 1), 0))
    lane_source, _ = place_of(lax.broadcasted_iota(jnp.int32, (1, chunk), 1))
    at_slot = lax.broadcasted_iota(jnp.int32, (chunk, 128), 1) == row_slot
    from_source = (lax.broadcasted_iota(jnp.int32, (max(per, 8), chunk), 0) == lane_source).astype(F32)
    key_rows = per * (tall if extra else rows)
    key_step, key_at = (tall, cap - rows) if extra else (rows, cap)
    key_pick = (
        lax.broadcasted_iota(jnp.int32, (chunk, key_rows), 1) == row_source * key_step + key_at
    ).astype(F32).astype(BF16)
    if extra:
        low = lax.broadcasted_iota(jnp.int32, (per * extra, per * tall), 0)
        high = lax.broadcasted_iota(jnp.int32, (per * extra, per * tall), 1)
        low = low // extra * tall + low % extra

    def group_best(buf, buf_x, sem, sem_x, send_first, to_group):
        best[...] = jnp.full_like(best, -1.0)

        def wait_source(q):
            @pl.when(q != me)
            def _():
                for copy in row_copies(q, buf, buf_x, sem, sem_x, 0, q):
                    copy.wait_recv()

        def pairs(ci, cj, both):
            ri = pl.ds(pl.multiple_of(ci * chunk, 16), chunk)
            rj = pl.ds(pl.multiple_of(cj * chunk, 16), chunk)
            scores = lax.dot_general(
                buf[ri, :], buf[rj, :], (((1,), (1,)), ((), ())), preferred_element_type=F32
            )
            ki = keycol[ri, 0:1]
            kj = keyrow[pl.ds(cj * 8, 1), 0:chunk]
            ii = lax.broadcasted_iota(jnp.int32, (chunk, chunk), 0) + (ci - cj) * chunk
            jj = lax.broadcasted_iota(jnp.int32, (chunk, chunk), 1)
            ok = (ki == kj) & (ii != jj)
            kept = jnp.where(ok, scores, -1.0)
            top = jnp.max(kept, axis=1, keepdims=True)
            best[ri, :] = jnp.maximum(best[ri, :], jnp.broadcast_to(top, (chunk, 128)))
            if both:
                down = jnp.broadcast_to(jnp.max(kept, axis=0, keepdims=True), (128, chunk))
                best[rj, :] = jnp.maximum(best[rj, :], jnp.transpose(down))

        my_chunk = lax.div(me, per)

        @pl.loop(0, chunks)
        def _(step):
            c = walk(my_chunk, step, chunks)

            @pl.loop(0, per)
            def _(j):
                wait_source(c * per + j)

            here = pl.ds(pl.multiple_of(c * chunk, 16), chunk)
            if extra:
                tiles = buf_x[pl.ds(pl.multiple_of(c * key_rows, key_rows), key_rows), :]
                for k in range(pieces):
                    gather = (high == low + k * extra).astype(F32).astype(BF16)
                    buf[pl.ds(pl.multiple_of(c * chunk + main, 16), per * extra), k * 128:(k + 1) * 128] = jnp.dot(
                        gather, tiles, preferred_element_type=F32
                    ).astype(BF16)
            else:
                tiles = buf[here, 0:128]
            lane_keys = jnp.dot(key_pick, tiles, preferred_element_type=F32)
            col = jnp.sum(jnp.where(at_slot, lane_keys, 0.0), axis=1, keepdims=True)
            cols = jnp.broadcast_to(col, (chunk, 128))
            keycol[here, :] = cols
            turned = jnp.transpose(cols)
            keyrow[pl.ds(pl.multiple_of(c * 8, 8), 8), 0:chunk] = jnp.where(turned[0:8, :] > 0.5, turned[0:8, :], -1.0)
            pairs(c, c, False)

            @pl.loop(0, step)
            def _(done):
                e = walk(my_chunk, done, chunks)
                pairs(c, e, True)

        @pl.loop(0, chunks)
        def _(c):
            here = pl.ds(pl.multiple_of(c * chunk, 16), chunk)
            lines = jnp.dot(
                from_source, jnp.where(at_slot, best[here, :], 0.0),
                preferred_element_type=F32, precision=lax.Precision.HIGHEST,
            )
            for j in range(per):
                resbuf[pl.ds(pl.multiple_of((send_first + c * per + j) * 8, 8), 1), :] = lines[j:j + 1, :]

            @pl.loop(0, per)
            def _(j):
                q = c * per + j

                @pl.when(q != me)
                def _():
                    result_copy(send_first, q, to_group).start()

                @pl.when(q == me)
                def _():
                    resrecv[pl.ds(pl.multiple_of(to_group * 8, 8), 8), :] = resbuf[
                        pl.ds(pl.multiple_of((send_first + q) * 8, 8), 8), :
                    ]

    def result_copy(send_first, q, group):
        return pltpu.make_async_remote_copy(
            src_ref=resbuf.at[pl.ds(pl.multiple_of((send_first + q) * 8, 8), 8)],
            dst_ref=resrecv.at[pl.ds(pl.multiple_of(group * 8, 8), 8)],
            send_sem=res_send_sem.at[send_first + q], recv_sem=res_recv_sem.at[group],
            device_id=coords(q), device_id_type=MESH,
        )

    @pl.when(is_holder)
    def _():
        group_best(giant, giant_x, giant_sem, giant_x_sem, devices, devices + my_owner)

    group_best(recv, recv_x, recv_sem, recv_x_sem, 0, me)

    @pl.loop(0, n_owner)
    def _(o):
        target, copies = giant_copies(o)

        @pl.when(target != me)
        def _():
            for copy in copies:
                copy.wait_send()

    @pl.loop(0, devices)
    def _(d):
        @pl.when(d != me)
        def _():
            for copy in local_copies(d):
                copy.wait_send()
            result_copy(0, d, me).wait_send()

            @pl.when(is_holder)
            def _():
                result_copy(devices, d, devices + my_owner).wait_send()

    @pl.loop(0, ndest)
    def _(g):
        o = g - devices
        source = jnp.where(g < devices, g, holder_split(o) * n_owner + o)

        @pl.when(source != me)
        def _():
            result_copy(0, me, g).wait_recv()

    lines = jnp.concatenate([resrecv[g * 8:g * 8 + 1, :] for g in range(ndest)], axis=0)
    if gpad > ndest:
        lines = jnp.concatenate([lines, jnp.zeros((gpad - ndest, 128), F32)], axis=0)
    dest_again = renumbered()
    hot = (lax.broadcasted_iota(jnp.int32, (gpad, shard), 0) == dest_again).astype(F32)
    found = lax.dot_general(
        lines, hot, (((0,), (0,)), ((), ())), preferred_element_type=F32, precision=lax.Precision.HIGHEST
    )
    out_ref[...] = jnp.sum(jnp.where(slot_hot > 0.5, found, 0.0), axis=0, keepdims=True)


def on_device(embeddings, row_dest, row_cluster):
    n_owner = lax.axis_size("owner")
    n_split = lax.axis_size("split")
    devices = n_owner * n_split
    ndest = devices + n_owner
    shard, width = embeddings.shape
    cap = max(2, 2 * shard // ndest)
    rows, extra = cap // 16 * 16, cap + 1 - cap // 16 * 16
    extra += extra % 2
    if rows == 0 or extra > 8 or extra * (width // 128) % 16:
        rows, extra = (cap + 1 + 15) // 16 * 16, 0
    tall = extra * (width // 128)
    per = 1
    while per * 2 <= devices and per * 2 * (rows + extra) <= 512:
        per *= 2
    chunk = per * (rows + extra)
    total = devices * (rows + extra)
    keep = max((ndest + 15) // 16 * 16, devices // per * 8)
    vmem = pl.BlockSpec(memory_space=pltpu.VMEM)
    tails = []
    if extra:
        tails = [
            pltpu.VMEM((ndest * tall, 128), BF16),
            pltpu.VMEM((devices * tall, 128), BF16),
            pltpu.VMEM((devices * tall, 128), BF16),
            pltpu.SemaphoreType.DMA((ndest,)),
            pltpu.SemaphoreType.DMA((devices,)),
            pltpu.SemaphoreType.DMA((devices,)),
        ]
    out = pl.pallas_call(
        functools.partial(kernel, (n_owner, n_split, cap, rows, extra, per)),
        out_shape=jax.ShapeDtypeStruct((1, shard), F32),
        in_specs=[vmem] * 3,
        out_specs=vmem,
        scratch_shapes=[
            pltpu.VMEM((shard, width), BF16),
            pltpu.VMEM((ndest * rows, width), BF16),
            pltpu.VMEM((total, width), BF16),
            pltpu.VMEM((total, width), BF16),
            pltpu.VMEM((total, 128), F32),
            pltpu.VMEM((keep, max(128, chunk)), F32),
            pltpu.VMEM((total, 128), F32),
            pltpu.VMEM((2 * devices * 8, 128), F32),
            pltpu.VMEM((ndest * 8, 128), F32),
            pltpu.SemaphoreType.DMA((ndest,)),
            pltpu.SemaphoreType.DMA((devices,)),
            pltpu.SemaphoreType.DMA((devices,)),
            pltpu.SemaphoreType.DMA((2 * devices,)),
            pltpu.SemaphoreType.DMA((ndest,)),
        ] + tails,
        compiler_params=pltpu.CompilerParams(
            collective_id=0, has_side_effects=True, vmem_limit_bytes=56 * 1024 * 1024
        ),
    )(embeddings, row_dest.reshape(1, shard), row_cluster.reshape(1, shard))
    return out.reshape(shard)


def solution(mesh):
    placed = (P(("owner", "split"), None), P(("owner", "split"), None), P(("owner", "split")))
    return jax.shard_map(
        on_device, mesh=mesh, in_specs=placed, out_specs=P(("owner", "split")), check_vma=False
    )
```
